256 devices in a mesh: coord: 64 (over x, z, core), dp: 4 (over y).
Axes of the slice: x: 4, y: 4, z: 8, core: 2. Of those that a mesh axis runs over, the one named last changes fastest.
Arguments:
- h_train: bfloat16 [2, 512, 256, 128], P(None, 'dp'), may hold values from -6 to 6
- gout_train: bfloat16 [2, 512, 256, 5120], P(None, 'dp', None, 'coord'), may hold values from -96 to 96
- h_val: bfloat16 [2, 64, 256, 128], P(None, 'dp'), may hold values from -6 to 6
- gout_val: bfloat16 [2, 64, 256, 5120], P(None, 'dp', None, 'coord'), may hold values from -96 to 96
- proj: bfloat16 [2, 5120, 128, 128], P(None, 'coord'), may hold values from -0.0390625 to 0.0390625
- bins: int32 [2, 5120], P(None, 'coord'), may hold values from 0 to 63
- tasks: int32 [64, 1], replicated, may hold values from 0 to 2
Outputs:
- cosines: float32 [512, 64], P('dp')
- scores: float32 [512, 3], P('dp')
The draws below stay inside these ranges and needn't reach their ends.
Inputs may be any that keep to these rules, and one draw needn't show every extreme that they name: `tasks`: every one of the 3 benchmarks has at least one validation example.
All inputs are finite; a program needn't handle non-finite values.
Results may differ from the reference program's by a relative error of at most 0.0003.
Values sent between devices are 32-bit elements; how exact they have to be, the bound alone decides.
No kernel may reach another device: no remote copies, remote signals or barrier semaphores. Data moves between devices by JAX's collectives and lax.ppermute only.
A program may use at most 128 MiB of HBM per device.

```python
import math
import jax
import jax.numpy as jnp
from jax import lax

DOUT = 5120
R = 128
KPROJ = 8192
BW = 128
LAYERS = 2
TOK = 256
NTASK = 3
NBIN = 64
TRAIN = 512
VAL = 64


def common_tokens(key, salt, width):
    return jax.random.normal(jax.random.fold_in(key, salt), (LAYERS, 1, TOK, width), jnp.float32)


def mixture(common, own, weight):
    return jnp.clip(weight * common + math.sqrt(1.0 - weight * weight) * own, -6.0, 6.0)


def draw_h_train(key, part):
    common = common_tokens(key, 501, R)
    key = jax.random.fold_in(key, 1)
    own = jax.random.normal(key, (LAYERS, TRAIN, TOK, R), jnp.float32)
    return mixture(common, own, 0.75).astype(jnp.bfloat16)


def draw_h_val(key, part):
    common = common_tokens(key, 501, R)
    key = jax.random.fold_in(key, 2)
    own = jax.random.normal(key, (LAYERS, VAL, TOK, R), jnp.float32)
    return mixture(common, own, 0.75).astype(jnp.bfloat16)


def draw_gout_train(key, part):
    common = common_tokens(key, 502, DOUT)
    key = jax.random.fold_in(key, 3)
    own = jax.random.normal(jax.random.fold_in(key, 7), (LAYERS, TRAIN, TOK, DOUT), jnp.float32)
    spread = jnp.exp(jax.random.uniform(jax.random.fold_in(key, 8), (LAYERS, TRAIN, 1, 1), jnp.float32, 0.0, math.log(10.0)))
    return (mixture(common, own, 0.75) * spread).astype(jnp.bfloat16)


def draw_gout_val(key, part):
    common = common_tokens(key, 502, DOUT)
    key = jax.random.fold_in(key, 4)
    own = jax.random.normal(jax.random.fold_in(key, 7), (LAYERS, VAL, TOK, DOUT), jnp.float32)
    spread = jnp.exp(jax.random.uniform(jax.random.fold_in(key, 8), (LAYERS, VAL, 1, 1), jnp.float32, 0.0, math.log(10.0)))
    return (mixture(common, own, 0.75) * spread).astype(jnp.bfloat16)


def with_ends(array, key, least, largest):
    index_at = [jax.random.randint(jax.random.fold_in(key, axis), (), 0, length) for axis, length in enumerate(array.shape)]
    main_axis = array.shape.index(max(array.shape))
    next_to = index_at[:main_axis] + [(index_at[main_axis] + 1) % array.shape[main_axis]] + index_at[main_axis + 1:]
    return array.at[tuple(index_at)].set(least).at[tuple(next_to)].set(largest)


def levels(rng, dims, pieces, low, high):
    level = 1.0
    for dim, shards_of in pieces:
        draws = jax.random.uniform(jax.random.fold_in(jax.random.fold_in(rng, 6), dim), (shards_of,), jnp.float32, low / len(pieces), high / len(pieces))
        level = level * jnp.repeat(jnp.exp(draws), dims[dim] // shards_of).reshape((-1,) + (1,) * (len(dims) - 1 - dim))
    return level


def distinct(stream_key, rows, amount, top, lift):
    sequence = jax.random.permutation(jax.random.fold_in(stream_key, 1), amount)
    favour = sequence
    for power in range(3):
        favour = favour * favour // amount
    favour = favour * lift // amount
    lots = jax.random.randint(jax.random.fold_in(stream_key, 2), (rows, amount), 0, 4096) + favour
    holders = jax.random.permutation(jax.random.fold_in(stream_key, 3), rows)[jnp.arange(amount) % rows]
    lots = jnp.where(jnp.arange(rows)[:, None] == holders[None, :], 1 << 14, lots)
    merit = lots * amount + jnp.arange(amount)
    return lax.top_k(merit.astype(jnp.int32), top)[1].astype(jnp.int32)


def noise(own_key, extent, scale, most, cuts=(), dtype=jnp.bfloat16):
    level = levels(own_key, extent, cuts, -0.22, 0.18) if cuts else 1.0
    array = jax.random.normal(own_key, extent, jnp.float32) * scale * level
    return jnp.minimum(jnp.maximum(array, -most), most).astype(dtype)


def setup_inputs(seed: int = 0) -> dict:
    arg_keys = jax.random.split(jax.random.key(seed), 8)
    return {
        "h_train": draw_h_train(jax.random.fold_in(arg_keys[7], 71), 0),
        "gout_train": draw_gout_train(jax.random.fold_in(arg_keys[7], 71), 0),
        "h_val": draw_h_val(jax.random.fold_in(arg_keys[7], 71), 0),
        "gout_val": draw_gout_val(jax.random.fold_in(arg_keys[7], 71), 0),
        "proj": noise(arg_keys[4], (LAYERS, DOUT, R, BW), (R * DOUT * LAYERS // NBIN) ** -0.5, 0.0390625, ((1, 64),)),
        "bins": with_ends(jax.random.randint(arg_keys[5], (LAYERS, DOUT), 0, NBIN), jax.random.fold_in(arg_keys[5], 1), 0, NBIN - 1).astype(jnp.int32),
        "tasks": distinct(arg_keys[6], VAL, NTASK, 1, 0),
    }


def features_of(h_all, g_all, proj, bins):
    total = jnp.zeros((h_all.shape[1], NBIN, BW), jnp.float32)
    for layer in range(LAYERS):
        weights = proj[layer].astype(jnp.float32)
        onehot = (bins[layer][:, None] == jnp.arange(NBIN)[None, :]).astype(jnp.float32)

        def one_example(pair):
            hx, gx = pair
            grads = jnp.dot(gx.T, hx, preferred_element_type=jnp.float32).astype(jnp.bfloat16)
            placed = jnp.einsum('jr,jrk->jk', grads.astype(jnp.float32), weights, precision=lax.Precision.HIGHEST)
            return jnp.dot(onehot.T, placed, precision=lax.Precision.HIGHEST)
        total = total + lax.map(one_example, (h_all[layer], g_all[layer]))
    return total.reshape(h_all.shape[1], KPROJ)

def reference(h_train, gout_train, h_val, gout_val, proj, bins, tasks):
    train_feats = features_of(h_train, gout_train, proj, bins)
    val_feats = features_of(h_val, gout_val, proj, bins)
    train_norm = jnp.sqrt(lax.optimization_barrier(jnp.sum(train_feats * train_feats, axis=1)) + 1e-06)
    val_norm = jnp.sqrt(lax.optimization_barrier(jnp.sum(val_feats * val_feats, axis=1)) + 1e-06)
    dots = jnp.dot(train_feats, val_feats.T, precision=lax.Precision.HIGHEST)
    cosines = dots / (train_norm[:, None] * val_norm[None, :])
    members = (tasks[:, 0][:, None] == jnp.arange(NTASK)[None, :]).astype(jnp.float32)
    scores = jnp.dot(cosines, members, precision=lax.Precision.HIGHEST) / lax.optimization_barrier(jnp.sum(members, axis=0))[None, :]
    return (cosines, scores)
```

```python
import functools

import jax
import jax.numpy as jnp
from jax import lax
from jax.experimental import pallas as pl
from jax.experimental.pallas import tpu as pltpu
from jax.sharding import PartitionSpec as P

BW = 128
NTASK = 3
NBIN = 64
NX, NZ, NC, NY = 4, 8, 2, 4
HALF = NBIN // NC


def coord_pairs(target):
    place = lambda x, z, c: (x * NZ + z) * NC + c
    return [
        (place(x, z, c), place(*target(x, z, c)))
        for x in range(NX)
        for z in range(NZ)
        for c in range(NC)
    ]


def to_core(a):
    return lax.ppermute(a, "coord", coord_pairs(lambda x, z, c: (x, z, 1 - c)))


def along_x(a, d):
    return lax.ppermute(a, "coord", coord_pairs(lambda x, z, c: ((x + d) % NX, z, c)))


def along_z(a, d):
    return lax.ppermute(a, "coord", coord_pairs(lambda x, z, c: (x, (z + d) % NZ, c)))


def z_partner(a):
    return lax.ppermute(a, "coord", coord_pairs(lambda x, z, c: (x, z ^ 1, c)))


def along_y(a, d):
    return lax.ppermute(a, "dp", [(y, (y + d) % NY) for y in range(NY)])


def place_of_device():
    i = lax.axis_index("coord")
    return i // (NZ * NC), (i // NC) % NZ, i % NC


def feature_kernel(cfg, bins, h_t, g_t, h_v, g_v, proj, out, hbuf, gbuf, pbuf, grads, sem_t, sem_v, sem_p):
    layers, n_t, n_v, cols, blk, unroll_a, unroll_b = cfg
    n = n_t + n_v
    nblk = n_t // blk

    def copies_t(l, b):
        s = pl.ds(b * blk, blk)
        return (
            pltpu.make_async_copy(h_t.at[l, s], hbuf.at[l, s], sem_t.at[0, l, b]),
            pltpu.make_async_copy(g_t.at[l, s], gbuf.at[l, s], sem_t.at[1, l, b]),
        )

    def copies_v(l):
        s = pl.ds(n_t, n_v)
        return (
            pltpu.make_async_copy(h_v.at[l], hbuf.at[l, s], sem_v.at[0, l]),
            pltpu.make_async_copy(g_v.at[l], gbuf.at[l, s], sem_v.at[1, l]),
        )

    def copy_p(l):
        return pltpu.make_async_copy(proj.at[l], pbuf.at[l], sem_p.at[l])

    for l in range(layers):
        for copy in copies_v(l):
            copy.start()
        for b in range(nblk):
            for copy in copies_t(l, b):
                copy.start()
        copy_p(l).start()

    @pl.loop(0, NBIN)
    def _(b):
        out[b] = jnp.zeros((n, BW), jnp.float32)

    my_x, my_z, my_c = place_of_device()

    def example(l, e):
        g = jnp.dot(gbuf[l, e], hbuf[l, e], preferred_element_type=jnp.float32)
        grads[pl.ds(e, cols, stride=n), :] = g

    for l in range(layers):
        for copy in copies_v(l):
            copy.wait()

        @pl.loop(n_t, n, unroll=unroll_a)
        def _(e):
            example(l, e)

        @pl.loop(0, nblk)
        def _(b):
            for copy in copies_t(l, b):
                copy.wait()

            @pl.loop(0, blk, unroll=unroll_a)
            def _(e):
                example(l, b * blk + e)

        copy_p(l).wait()

        @pl.loop(0, cols, unroll=unroll_b)
        def _(j):
            a = grads[pl.ds(j * n, n), :].astype(jnp.bfloat16)
            p = jnp.dot(a, pbuf[l, j], preferred_element_type=jnp.float32)
            b = bins[l, j]
            far_c = (b // HALF) ^ my_c
            far_x = ((b // NZ) - my_x) & (NX - 1)
            far_z = (b - my_z) & (NZ - 1)
            out[far_c * HALF + far_x * NZ + far_z] += p


def local_features(bins, h_t, g_t, h_v, g_v, proj):
    layers, n_t, tok, r = h_t.shape
    n_v, cols = h_v.shape[1], g_t.shape[2]
    n = n_t + n_v
    blk = 16
    any_space = pl.BlockSpec(memory_space=pl.ANY)
    return pl.pallas_call(
        functools.partial(feature_kernel, (layers, n_t, n_v, cols, blk, 16, 16)),
        out_shape=jax.ShapeDtypeStruct((NBIN, n, BW), jnp.float32),
        in_specs=[pl.BlockSpec(memory_space=pltpu.SMEM)] + [any_space] * 5,
        out_specs=pl.BlockSpec(memory_space=pltpu.VMEM),
        scratch_shapes=[
            pltpu.VMEM((layers, n, tok, r), jnp.bfloat16),
            pltpu.VMEM((layers, n, cols, tok), jnp.bfloat16),
            pltpu.VMEM((layers, cols, r, BW), jnp.bfloat16),
            pltpu.VMEM((cols * n, r), jnp.float32),
            pltpu.SemaphoreType.DMA((2, layers, n_t // blk)),
            pltpu.SemaphoreType.DMA((2, layers)),
            pltpu.SemaphoreType.DMA((layers,)),
        ],
        compiler_params=pltpu.CompilerParams(vmem_limit_bytes=56 * 1024 * 1024),
        name="features",
    )(bins, h_t, g_t, h_v, g_v, proj)


def reduce_to_owner(f):
    half = {}
    for d in (2, 1, 3, 0):
        far = to_core(f[HALF + d * NZ : HALF + (d + 1) * NZ])
        half[d] = f[d * NZ : (d + 1) * NZ] + far
    mid = NZ // 2
    right = along_x(half[2][:mid], 1)
    left = along_x(half[2][mid:], -1)
    right = along_x(jnp.concatenate([half[1][:mid] + right, half[1][mid:]]), 1)
    left = along_x(jnp.concatenate([half[3][:mid], half[3][mid:] + left]), -1)
    own = half[0] + right + left
    got = [along_z(own[d], d) for d in (4, 3, 5, 2, 6, 1, 7)]
    total = own[0]
    for part in got:
        total = total + part
    return total


def dots_kernel(n_t, n_v, total, v1, v2, v3, keep, send, val, dots, stats):
    y = lax.axis_index("dp")
    _, _, c = place_of_device()
    train = total[0:n_t, :]
    val[pl.ds(pl.multiple_of(y * n_v, n_v), n_v), :] = total[n_t : n_t + n_v, :]
    for d, part in ((1, v1), (2, v2), (3, v3)):
        val[pl.ds(pl.multiple_of(((y - d) & (NY - 1)) * n_v, n_v), n_v), :] = part[...]
    v = val[...]
    contract = lambda a, b: lax.dot_general(
        a, b, (((1,), (1,)), ((), ())), precision=lax.Precision.HIGHEST, preferred_element_type=jnp.float32
    )
    dots[...] = contract(v, train)
    ones = jnp.ones((8, BW), jnp.float32)
    stats[0] = contract(ones, train * train)
    stats[1] = jnp.zeros_like(stats[1])
    stats[1, :, 0 : NY * n_v] = contract(ones, v * v)
    rows = NY * n_v // NC
    for ref, h in ((keep, c), (send, 1 - c)):
        ref[0:rows, :] = dots[pl.ds(pl.multiple_of(h * rows, rows), rows), :]
        ref[rows : rows + 8, :] = stats[h]


def scores_kernel(mine, other, tasks, cos_out, score_out, dots, stats):
    _, _, c = place_of_device()
    n_v = tasks.shape[1]
    rows = n_v // NC
    for ref, h in ((mine, c), (other, 1 - c)):
        dots[pl.ds(pl.multiple_of(h * rows, rows), rows), :] = ref[0:rows, :]
        stats[h] = ref[rows : rows + 8, :]
    on_diagonal = lax.broadcasted_iota(jnp.int32, (n_v, n_v), 0) == lax.broadcasted_iota(jnp.int32, (n_v, n_v), 1)
    train_norm = jnp.sqrt(stats[0, 0:1, :] + 1e-06)
    val_norm_row = jnp.sqrt(stats[1, 0:1, 0:n_v] + 1e-06)
    val_norm = jnp.sum(jnp.where(on_diagonal, val_norm_row, 0.0), axis=1, keepdims=True)
    cos = dots[...] / (train_norm * val_norm)
    cos_out[...] = cos
    task_row = tasks[...].astype(jnp.float32)
    task = jnp.sum(jnp.where(on_diagonal, task_row, 0.0), axis=1, keepdims=True)
    for s in range(NTASK):
        member = (task == float(s)).astype(jnp.float32)
        count = jnp.sum(member, axis=0, keepdims=True)
        score_out[s : s + 1, :] = jnp.sum(cos * member, axis=0, keepdims=True) / count


def per_device(h_train, gout_train, h_val, gout_val, proj, bins, tasks):
    n_t, n_v = h_train.shape[1], h_val.shape[1]
    all_v = n_v * NY
    f = local_features(
        bins, h_train, jnp.swapaxes(gout_train, 2, 3), h_val, jnp.swapaxes(gout_val, 2, 3), proj
    )
    total = reduce_to_owner(f)
    v = total[n_t:]
    others = [along_y(v, d) for d in (1, 2, 3)]
    part = jax.ShapeDtypeStruct((all_v // NC + 8, n_t), jnp.float32)
    keep, send = pl.pallas_call(
        functools.partial(dots_kernel, n_t, n_v),
        out_shape=(part, part),
        scratch_shapes=[
            pltpu.VMEM((all_v, BW), jnp.float32),
            pltpu.VMEM((all_v, n_t), jnp.float32),
            pltpu.VMEM((NC, 8, n_t), jnp.float32),
        ],
        name="dots",
    )(total, *others)
    a = keep + to_core(send)
    got = [along_x(a, d) for d in (2, 1, 3)]
    a = a + got[0] + got[1] + got[2]
    a = a + z_partner(a)
    got = [along_z(a, d) for d in (4, 2, 6)]
    a = a + got[0] + got[1] + got[2]
    cos_t, scores_t = pl.pallas_call(
        scores_kernel,
        out_shape=(
            jax.ShapeDtypeStruct((all_v, n_t), jnp.float32),
            jax.ShapeDtypeStruct((NTASK, n_t), jnp.float32),
        ),
        scratch_shapes=[
            pltpu.VMEM((all_v, n_t), jnp.float32),
            pltpu.VMEM((NC, 8, n_t), jnp.float32),
        ],
        name="scores",
    )(a, to_core(a), tasks.reshape(1, all_v))
    return cos_t.T, scores_t.T


def solution(mesh):
    in_specs = (
        P(None, "dp", None, None),
        P(None, "dp", None, "coord"),
        P(None, "dp", None, None),
        P(None, "dp", None, "coord"),
        P(None, "coord", None, None),
        P(None, "coord"),
        P(),
    )
    out_specs = (P("dp", None), P("dp", None))
    return jax.shard_map(
        per_device, mesh=mesh, in_specs=in_specs, out_specs=out_specs, check_vma=False
    )
```

```python
import functools

import jax
import jax.numpy as jnp
from jax import lax
from jax.experimental import pallas as pl
from jax.experimental.pallas import tpu as pltpu
from jax.sharding import PartitionSpec as P

BW = 128
NTASK = 3
NBIN = 64
NX, NZ, NC, NY = 4, 8, 2, 4
HALF = NBIN // NC
ROWS_B = 16


def coord_pairs(target):
    place = lambda x, z, c: (x * NZ + z) * NC + c
    return [
        (place(x, z, c), place(*target(x, z, c)))
        for x in range(NX)
        for z in range(NZ)
        for c in range(NC)
    ]


def to_core(a):
    return lax.ppermute(a, "coord", coord_pairs(lambda x, z, c: (x, z, 1 - c)))


def along_x(a, d):
    return lax.ppermute(a, "coord", coord_pairs(lambda x, z, c: ((x + d) % NX, z, c)))


def along_z(a, d):
    return lax.ppermute(a, "coord", coord_pairs(lambda x, z, c: (x, (z + d) % NZ, c)))


def z_partner(a):
    return lax.ppermute(a, "coord", coord_pairs(lambda x, z, c: (x, z ^ 1, c)))


def along_y(a, d):
    return lax.ppermute(a, "dp", [(y, (y + d) % NY) for y in range(NY)])


def place_of_device():
    i = lax.axis_index("coord")
    return i // (NZ * NC), (i // NC) % NZ, i % NC


def feature_kernel(cfg, bins_hbm, h_t, g_t, h_v, g_v, proj, out_a, out_b, h_buf, g_buf, hv_buf, gv_buf, p_buf, grads, bins, sem_t, sem_v, sem_p, sem_b):
    layers, n_t, n_v, cols, blk, slots, unroll = cfg
    n = n_t + n_v
    n_a = out_a.shape[1]
    nblk = n_t // blk
    share = cols // nblk

    def train_copies(t):
        l, s = t // nblk, pl.ds((t % nblk) * blk, blk)
        at = t % slots
        return (
            pltpu.make_async_copy(h_t.at[l, s], h_buf.at[at], sem_t.at[0, at]),
            pltpu.make_async_copy(g_t.at[l, s], g_buf.at[at], sem_t.at[1, at]),
        )

    def val_copies(l):
        return (
            pltpu.make_async_copy(h_v.at[l], hv_buf.at[l], sem_v.at[0, l]),
            pltpu.make_async_copy(g_v.at[l], gv_buf.at[l], sem_v.at[1, l]),
        )

    def proj_copy(l):
        return pltpu.make_async_copy(proj.at[l], p_buf.at[l], sem_p.at[l])

    def start(copies):
        for copy in copies:
            copy.start()

    def wait(copies):
        for copy in copies:
            copy.wait()

    bins_copy = pltpu.make_async_copy(bins_hbm, bins, sem_b)
    bins_copy.start()
    for t in range(slots):
        start(train_copies(t))
        if t == 1:
            start(val_copies(0))
    proj_copy(0).start()

    @pl.loop(0, NBIN)
    def _(b):
        out_a[b] = jnp.zeros(out_a.shape[1:], jnp.float32)
        out_b[b] = jnp.zeros(out_b.shape[1:], jnp.float32)

    bins_copy.wait()
    my_x, my_z, my_c = place_of_device()

    def example(l, g, h, e):
        grads[l, pl.ds(e, cols, stride=n), :] = jnp.dot(g, h, preferred_element_type=jnp.float32)

    def project(l, j):
        a = grads[l, pl.ds(j * n, n), :].astype(jnp.bfloat16)
        p = jnp.dot(a, p_buf[l, j], preferred_element_type=jnp.float32)
        b = bins[l, j]
        far_c = (b // HALF) ^ my_c
        far_odd = (b ^ my_z) & 1
        far_quad = ((b - (my_z ^ far_odd)) & (NZ - 1)) // 2
        far_x = ((b // NZ) - my_x) & (NX - 1)
        slot_a = ((far_x + 2) & (NX - 1)) * NZ + far_odd * (NZ // 2) + far_quad
        slot_b = far_odd * (HALF // 2) + far_quad * NX + far_x
        out_a[far_c * HALF + slot_a] += p[:n_a]
        out_b[far_c * HALF + slot_b] += p[n_a:]

    for l in range(layers):

        @pl.loop(0, nblk)
        def _(b):
            t = l * nblk + b
            wait(train_copies(t))
            at = t % slots
            for i in range(blk):
                example(l, g_buf[at, i], h_buf[at, i], b * blk + i)
            if l > 0:
                for i in range(share):
                    project(l - 1, b * share + i)

            @pl.when(t + slots < layers * nblk)
            def _():
                start(train_copies(t + slots))

            if l + 1 < layers:

                @pl.when(b == nblk // 2)
                def _():
                    start(val_copies(l + 1))
                    proj_copy(l + 1).start()

        wait(val_copies(l))
        for i in range(n_v):
            example(l, gv_buf[l, i], hv_buf[l, i], n_t + i)
        proj_copy(l).wait()

    @pl.loop(0, cols, unroll=unroll)
    def _(j):
        project(layers - 1, j)


def local_features(bins, h_t, g_t, h_v, g_v, proj, n_a):
    layers, n_t, tok, r = h_t.shape
    n_v, cols = h_v.shape[1], g_t.shape[2]
    n = n_t + n_v
    blk, slots, unroll = 16, 6, 20
    in_hbm = pl.BlockSpec(memory_space=pltpu.HBM)
    return pl.pallas_call(
        functools.partial(feature_kernel, (layers, n_t, n_v, cols, blk, slots, unroll)),
        out_shape=(
            pltpu.VMEM((NBIN, n_a, BW), jnp.float32),
            pltpu.VMEM((NBIN, n - n_a, BW), jnp.float32),
        ),
        in_specs=[in_hbm] * 6,
        out_specs=[pl.BlockSpec(memory_space=pltpu.VMEM)] * 2,
        scratch_shapes=[
            pltpu.VMEM((slots, blk, tok, r), jnp.bfloat16),
            pltpu.VMEM((slots, blk, cols, tok), jnp.bfloat16),
            pltpu.VMEM((layers, n_v, tok, r), jnp.bfloat16),
            pltpu.VMEM((layers, n_v, cols, tok), jnp.bfloat16),
            pltpu.VMEM((layers, cols, r, BW), jnp.bfloat16),
            pltpu.VMEM((layers, cols * n, r), jnp.float32),
            pltpu.SMEM((layers, cols), jnp.int32),
            pltpu.SemaphoreType.DMA((2, slots)),
            pltpu.SemaphoreType.DMA((2, layers)),
            pltpu.SemaphoreType.DMA((layers,)),
            pltpu.SemaphoreType.DMA,
        ],
        compiler_params=pltpu.CompilerParams(vmem_limit_bytes=42 * 1024 * 1024),
        name="features",
    )(*[pltpu.with_memory_space_constraint(a, pltpu.HBM) for a in (bins, h_t, g_t, h_v, g_v, proj)])


def in_vmem(a):
    return pltpu.with_memory_space_constraint(a, pltpu.VMEM)


def add(parts):
    total = parts[0]
    for part in parts[1:]:
        total = total + part
    return total


def along_z_pairs(a):
    return add([a[0]] + [along_z(a[d], 2 * d) for d in (2, 1, 3)])


def reduce_to_owner(f_a, f_b):
    mid = NZ // 2
    first = to_core(f_a[HALF : HALF + NZ])
    first, rest, far_b = lax.optimization_barrier((first, f_a[HALF + NZ :], f_b[HALF:]))
    far_b, rest = to_core(far_b), to_core(rest)
    half = f_a[:NZ] + first
    right, left = along_x(half[:mid], 1), along_x(half[mid:], -1)
    b = f_b[:HALF] + far_b
    far_b = z_partner(b[HALF // 2 :])
    right, left, rest = lax.optimization_barrier((right, left, rest))
    half = f_a[NZ:HALF] + rest
    right = along_x(jnp.concatenate([half[2 * NZ : 2 * NZ + mid] + right, half[2 * NZ + mid :]]), 1)
    left = along_x(jnp.concatenate([half[:mid], half[mid:NZ] + left]), -1)
    b = (b[: HALF // 2] + far_b).reshape(mid, NX, *b.shape[1:])
    b = along_z_pairs(b)
    a = half[NZ : 2 * NZ] + right + left
    a = a[:mid] + z_partner(a[mid:])
    b = add([b[0]] + [along_x(b[d], d) for d in (2, 1, 3)])
    return along_z_pairs(a), b


def dots_kernel(n_v, rows_a, rows_b, v1, v2, v3, keep, send, val, dots, stats):
    y = lax.axis_index("dp")
    _, _, c = place_of_device()
    n_b = rows_b.shape[0]
    train = rows_a[...]
    if n_b > n_v:
        train = jnp.concatenate([train, rows_b[0 : n_b - n_v, :]])
    val[pl.ds(pl.multiple_of(y * n_v, n_v), n_v), :] = rows_b[n_b - n_v : n_b, :]
    for d, part in ((1, v1), (2, v2), (3, v3)):
        val[pl.ds(pl.multiple_of(((y - d) & (NY - 1)) * n_v, n_v), n_v), :] = part[...]
    v = val[...]
    contract = lambda a, b: lax.dot_general(
        a, b, (((1,), (1,)), ((), ())), precision=lax.Precision.HIGHEST, preferred_element_type=jnp.float32
    )
    dots[...] = contract(v, train)
    ones = jnp.ones((8, BW), jnp.float32)
    stats[0] = contract(ones, train * train)
    stats[1] = jnp.zeros_like(stats[1])
    stats[1, :, 0 : NY * n_v] = contract(ones, v * v)
    rows = NY * n_v // NC
    for ref, h in ((keep, c), (send, 1 - c)):
        ref[0:rows, :] = dots[pl.ds(pl.multiple_of(h * rows, rows), rows), :]
        ref[rows : rows + 8, :] = stats[h]


def scores_kernel(mine, other, tasks, cos_out, score_out, dots, stats):
    _, _, c = place_of_device()
    n_v = tasks.shape[1]
    rows = n_v // NC
    for ref, h in ((mine, c), (other, 1 - c)):
        dots[pl.ds(pl.multiple_of(h * rows, rows), rows), :] = ref[0:rows, :]
        stats[h] = ref[rows : rows + 8, :]
    on_diagonal = lax.broadcasted_iota(jnp.int32, (n_v, n_v), 0) == lax.broadcasted_iota(jnp.int32, (n_v, n_v), 1)
    train_norm = jnp.sqrt(stats[0, 0:1, :] + 1e-06)
    val_norm_row = jnp.sqrt(stats[1, 0:1, 0:n_v] + 1e-06)
    val_norm = jnp.sum(jnp.where(on_diagonal, val_norm_row, 0.0), axis=1, keepdims=True)
    cos = dots[...] / (train_norm * val_norm)
    cos_out[...] = cos
    task_row = tasks[...].astype(jnp.float32)
    task = jnp.sum(jnp.where(on_diagonal, task_row, 0.0), axis=1, keepdims=True)
    for s in range(NTASK):
        member = (task == float(s)).astype(jnp.float32)
        count = jnp.sum(member, axis=0, keepdims=True)
        score_out[s : s + 1, :] = jnp.sum(cos * member, axis=0, keepdims=True) / count


def per_device(h_train, gout_train, h_val, gout_val, proj, bins, tasks):
    n_t, n_v = h_train.shape[1], h_val.shape[1]
    all_v = n_v * NY
    n_a = n_t - ROWS_B
    f_a, f_b = local_features(
        bins, h_train, jnp.swapaxes(gout_train, 2, 3), h_val, jnp.swapaxes(gout_val, 2, 3), proj, n_a
    )
    rows_a, rows_b = reduce_to_owner(f_a, f_b)
    v = rows_b[ROWS_B:]
    others = [along_y(v, d) for d in (1, 2, 3)]
    part = pltpu.VMEM((all_v // NC + 8, n_t), jnp.float32)
    keep, send = pl.pallas_call(
        functools.partial(dots_kernel, n_v),
        out_shape=(part, part),
        scratch_shapes=[
            pltpu.VMEM((all_v, BW), jnp.float32),
            pltpu.VMEM((all_v, n_t), jnp.float32),
            pltpu.VMEM((NC, 8, n_t), jnp.float32),
        ],
        name="dots",
    )(*map(in_vmem, (rows_a, rows_b, *others)))
    a = keep + to_core(send)
    got = [along_x(a, d) for d in (2, 1, 3)]
    a = a + got[0] + got[1] + got[2]
    a = a + z_partner(a)
    a = add([a] + [along_z(a, d) for d in (4, 2, 6)])
    cos_t, scores_t = pl.pallas_call(
        scores_kernel,
        out_shape=(
            jax.ShapeDtypeStruct((all_v, n_t), jnp.float32),
            jax.ShapeDtypeStruct((NTASK, n_t), jnp.float32),
        ),
        scratch_shapes=[
            pltpu.VMEM((all_v, n_t), jnp.float32),
            pltpu.VMEM((NC, 8, n_t), jnp.float32),
        ],
        name="scores",
    )(in_vmem(a), in_vmem(to_core(a)), tasks.reshape(1, all_v))
    return cos_t.T, scores_t.T


def solution(mesh):
    in_specs = (
        P(None, "dp", None, None),
        P(None, "dp", None, "coord"),
        P(None, "dp", None, None),
        P(None, "dp", None, "coord"),
        P(None, "coord", None, None),
        P(None, "coord"),
        P(),
    )
    out_specs = (P("dp", None), P("dp", None))
    return jax.shard_map(
        per_device, mesh=mesh, in_specs=in_specs, out_specs=out_specs, check_vma=False
    )
```

```python
import functools

import jax
import jax.numpy as jnp
from jax import lax
from jax.experimental import pallas as pl
from jax.experimental.pallas import tpu as pltpu
from jax.sharding import PartitionSpec as P

BW = 128
NTASK = 3
NBIN = 64
NX, NZ, NC, NY = 4, 8, 2, 4
HALF = NBIN // NC
ROWS_B = 16


def coord_pairs(target):
    place = lambda x, z, c: (x * NZ + z) * NC + c
    return [
        (place(x, z, c), place(*target(x, z, c)))
        for x in range(NX)
        for z in range(NZ)
        for c in range(NC)
    ]


def to_core(a):
    return lax.ppermute(a, "coord", coord_pairs(lambda x, z, c: (x, z, 1 - c)))


def along_x(a, d):
    return lax.ppermute(a, "coord", coord_pairs(lambda x, z, c: ((x + d) % NX, z, c)))


def swap_x(a, d):
    return lax.ppermute(a, "coord", coord_pairs(lambda x, z, c: (x ^ d, z, c)))


def swap_z(a, d):
    return lax.ppermute(a, "coord", coord_pairs(lambda x, z, c: (x, z ^ d, c)))


def swap_y(a, d):
    return lax.ppermute(a, "dp", [(y, y ^ d) for y in range(NY)])


def place_of_device():
    i = lax.axis_index("coord")
    return i // (NZ * NC), (i // NC) % NZ, i % NC


def feature_kernel(cfg, bins_hbm, h_t, g_t, h_v, g_v, proj, out_a, out_b, h_buf, g_buf, hv_buf, gv_buf, p_buf, grads, bins, sem_t, sem_v, sem_p, sem_b):
    layers, n_t, n_v, cols, blk, slots, unroll = cfg
    n = n_t + n_v
    n_a = out_a.shape[1]
    nblk = n_t // blk
    share = cols // nblk

    def train_copies(t):
        l, s = t // nblk, pl.ds((t % nblk) * blk, blk)
        at = t % slots
        return (
            pltpu.make_async_copy(h_t.at[l, s], h_buf.at[at], sem_t.at[0, at]),
            pltpu.make_async_copy(g_t.at[l, s], g_buf.at[at], sem_t.at[1, at]),
        )

    def val_copies(l):
        return (
            pltpu.make_async_copy(h_v.at[l], hv_buf.at[l], sem_v.at[0, l]),
            pltpu.make_async_copy(g_v.at[l], gv_buf.at[l], sem_v.at[1, l]),
        )

    def proj_copy(l):
        return pltpu.make_async_copy(proj.at[l], p_buf.at[l], sem_p.at[l])

    def start(copies):
        for copy in copies:
            copy.start()

    def wait(copies):
        for copy in copies:
            copy.wait()

    bins_copy = pltpu.make_async_copy(bins_hbm, bins, sem_b)
    bins_copy.start()
    for t in range(slots):
        start(train_copies(t))
        if t == 1:
            start(val_copies(0))
    proj_copy(0).start()

    @pl.loop(0, NBIN)
    def _(b):
        out_a[b] = jnp.zeros(out_a.shape[1:], jnp.float32)
        out_b[b] = jnp.zeros(out_b.shape[1:], jnp.float32)

    bins_copy.wait()
    my_x, my_z, my_c = place_of_device()

    def example(l, g, h, e):
        grads[l, pl.ds(e, cols, stride=n), :] = jnp.dot(g, h, preferred_element_type=jnp.float32)

    def project(l, j):
        a = grads[l, pl.ds(j * n, n), :].astype(jnp.bfloat16)
        p = jnp.dot(a, p_buf[l, j], preferred_element_type=jnp.float32)
        b = bins[l, j]
        far_c = (b // HALF) ^ my_c
        far_z = (b ^ my_z) & (NZ - 1)
        far_z = ((far_z ^ ((far_z >> 2) & ~(far_z >> 1))) & 1) * (NZ // 2) + far_z // 2
        b_x = b // NZ
        slot_a = ((b_x - my_x + 2) & (NX - 1)) * NZ + far_z
        slot_b = far_z * NX + ((b_x ^ my_x) & (NX - 1))
        out_a[far_c * HALF + slot_a] += p[:n_a]
        out_b[far_c * HALF + slot_b] += p[n_a:]

    for l in range(layers):

        @pl.loop(0, nblk)
        def _(b):
            t = l * nblk + b
            wait(train_copies(t))
            at = t % slots
            for i in range(blk):
                example(l, g_buf[at, i], h_buf[at, i], b * blk + i)
            if l > 0:
                for i in range(share):
                    project(l - 1, b * share + i)

            @pl.when(t + slots < layers * nblk)
            def _():
                start(train_copies(t + slots))

            if l + 1 < layers:

                @pl.when(b == nblk // 2)
                def _():
                    start(val_copies(l + 1))
                    proj_copy(l + 1).start()

        wait(val_copies(l))
        for i in range(n_v):
            example(l, gv_buf[l, i], hv_buf[l, i], n_t + i)
        proj_copy(l).wait()

    @pl.loop(0, cols, unroll=unroll)
    def _(j):
        project(layers - 1, j)


def local_features(bins, h_t, g_t, h_v, g_v, proj, n_a):
    layers, n_t, tok, r = h_t.shape
    n_v, cols = h_v.shape[1], g_t.shape[2]
    n = n_t + n_v
    blk, slots, unroll = 16, 6, 40
    in_hbm = pl.BlockSpec(memory_space=pltpu.HBM)
    return pl.pallas_call(
        functools.partial(feature_kernel, (layers, n_t, n_v, cols, blk, slots, unroll)),
        out_shape=(
            pltpu.VMEM((NBIN, n_a, BW), jnp.float32),
            pltpu.VMEM((NBIN, n - n_a, BW), jnp.float32),
        ),
        in_specs=[in_hbm] * 6,
        out_specs=[pl.BlockSpec(memory_space=pltpu.VMEM)] * 2,
        scratch_shapes=[
            pltpu.VMEM((slots, blk, tok, r), jnp.bfloat16),
            pltpu.VMEM((slots, blk, cols, tok), jnp.bfloat16),
            pltpu.VMEM((layers, n_v, tok, r), jnp.bfloat16),
            pltpu.VMEM((layers, n_v, cols, tok), jnp.bfloat16),
            pltpu.VMEM((layers, cols, r, BW), jnp.bfloat16),
            pltpu.VMEM((layers, cols * n, r), jnp.float32),
            pltpu.SMEM((layers, cols), jnp.int32),
            pltpu.SemaphoreType.DMA((2, slots)),
            pltpu.SemaphoreType.DMA((2, layers)),
            pltpu.SemaphoreType.DMA((layers,)),
            pltpu.SemaphoreType.DMA,
        ],
        compiler_params=pltpu.CompilerParams(vmem_limit_bytes=42 * 1024 * 1024),
        name="features",
    )(*[pltpu.with_memory_space_constraint(a, pltpu.HBM) for a in (bins, h_t, g_t, h_v, g_v, proj)])


def in_vmem(a):
    return pltpu.with_memory_space_constraint(a, pltpu.VMEM)


def add(parts):
    total = parts[0]
    for part in parts[1:]:
        total = total + part
    return total


def sum_quad(a):
    return add([a[0]] + [swap_z(a[i], d) for i, d in ((2, 5), (1, 2), (3, 6))])


def reduce_to_owner(f_a, f_b):
    mid = NZ // 2
    first = to_core(f_a[HALF : HALF + NZ])
    first, rest, far_b = lax.optimization_barrier((first, f_a[HALF + NZ :], f_b[HALF:]))
    far_b, rest = to_core(far_b), to_core(rest)
    half = f_a[:NZ] + first
    right, left = along_x(half[:mid], 1), along_x(half[mid:], -1)
    b = f_b[:HALF] + far_b
    far_b = swap_z(b[HALF // 2 :], 1)
    right, left, rest = lax.optimization_barrier((right, left, rest))
    half = f_a[NZ:HALF] + rest
    right = along_x(jnp.concatenate([half[2 * NZ : 2 * NZ + mid] + right, half[2 * NZ + mid :]]), 1)
    left = along_x(jnp.concatenate([half[:mid], half[mid:NZ] + left]), -1)
    b = (b[: HALF // 2] + far_b).reshape(mid, NX, *b.shape[1:])
    b = sum_quad(b)
    a = half[NZ : 2 * NZ] + right + left
    a = a[:mid] + swap_z(a[mid:], 1)
    b = add([b[0]] + [swap_x(b[d], d) for d in (2, 1, 3)])
    return sum_quad(a), b


def dots_kernel(n_v, rows_a, rows_b, v1, v2, v3, out, val):
    y = lax.axis_index("dp")
    n_b = rows_b.shape[0]
    all_v = NY * n_v
    train = rows_a[...]
    if n_b > n_v:
        train = jnp.concatenate([train, rows_b[0 : n_b - n_v, :]])
    val[pl.ds(pl.multiple_of(y * n_v, n_v), n_v), :] = rows_b[n_b - n_v : n_b, :]
    for d, part in ((1, v1), (2, v2), (3, v3)):
        val[pl.ds(pl.multiple_of((y ^ d) * n_v, n_v), n_v), :] = part[...]
    v = val[...]
    contract = lambda a, b: lax.dot_general(
        a, b, (((1,), (1,)), ((), ())), precision=lax.Precision.HIGHEST, preferred_element_type=jnp.float32
    )
    out[0:all_v, :] = contract(v, train)
    ones = jnp.ones((8, BW), jnp.float32)
    out[all_v : all_v + 8, :] = contract(ones, train * train)
    out[all_v + 8 : all_v + 16, :] = jnp.zeros((8, out.shape[1]), jnp.float32)
    out[all_v + 8 : all_v + 16, 0:all_v] = contract(ones, v * v)


def scores_kernel(*refs):
    *parts, tasks, cos_out, score_out = refs
    n_v = tasks.shape[1]
    total = add([part[...] for part in parts])
    on_diagonal = lax.broadcasted_iota(jnp.int32, (n_v, n_v), 0) == lax.broadcasted_iota(jnp.int32, (n_v, n_v), 1)
    train_norm = jnp.sqrt(total[n_v : n_v + 1, :] + 1e-06)
    val_norm_row = jnp.sqrt(total[n_v + 8 : n_v + 9, 0:n_v] + 1e-06)
    val_norm = jnp.sum(jnp.where(on_diagonal, val_norm_row, 0.0), axis=1, keepdims=True)
    cos = total[0:n_v, :] / (train_norm * val_norm)
    cos_out[...] = cos
    task_row = tasks[...].astype(jnp.float32)
    task = jnp.sum(jnp.where(on_diagonal, task_row, 0.0), axis=1, keepdims=True)
    for s in range(NTASK):
        member = (task == float(s)).astype(jnp.float32)
        count = jnp.sum(member, axis=0, keepdims=True)
        score_out[s : s + 1, :] = jnp.sum(cos * member, axis=0, keepdims=True) / count


def per_device(h_train, gout_train, h_val, gout_val, proj, bins, tasks):
    n_t, n_v = h_train.shape[1], h_val.shape[1]
    all_v = n_v * NY
    n_a = n_t - ROWS_B
    f_a, f_b = local_features(
        bins, h_train, jnp.swapaxes(gout_train, 2, 3), h_val, jnp.swapaxes(gout_val, 2, 3), proj, n_a
    )
    rows_a, rows_b = reduce_to_owner(f_a, f_b)
    v = rows_b[ROWS_B:]
    others = [swap_y(v, d) for d in (1, 2, 3)]
    a = pl.pallas_call(
        functools.partial(dots_kernel, n_v),
        out_shape=pltpu.VMEM((all_v + 16, n_t), jnp.float32),
        scratch_shapes=[pltpu.VMEM((all_v, BW), jnp.float32)],
        name="dots",
    )(*map(in_vmem, (rows_a, rows_b, *others)))
    a = add([a] + [swap_x(a, d) for d in (2, 1, 3)])
    a = add([a] + [swap_z(a, d) for d in (3, 2, 1)])
    a = a + swap_z(a, 6)
    parts = (a, to_core(a))
    cos_t, scores_t = pl.pallas_call(
        scores_kernel,
        out_shape=(
            jax.ShapeDtypeStruct((all_v, n_t), jnp.float32),
            jax.ShapeDtypeStruct((NTASK, n_t), jnp.float32),
        ),
        name="scores",
    )(*map(in_vmem, parts), tasks.reshape(1, all_v))
    return cos_t.T, scores_t.T


def solution(mesh):
    in_specs = (
        P(None, "dp", None, None),
        P(None, "dp", None, "coord"),
        P(None, "dp", None, None),
        P(None, "dp", None, "coord"),
        P(None, "coord", None, None),
        P(None, "coord"),
        P(),
    )
    out_specs = (P("dp", None), P("dp", None))
    return jax.shard_map(
        per_device, mesh=mesh, in_specs=in_specs, out_specs=out_specs, check_vma=False
    )
```

```python
import functools

import jax
import jax.numpy as jnp
from jax import lax
from jax.experimental import pallas as pl
from jax.experimental.pallas import tpu as pltpu
from jax.sharding import PartitionSpec as P

BW = 128
NTASK = 3
NBIN = 64
NX, NZ, NC, NY = 4, 8, 2, 4
HALF = NBIN // NC
ROWS_B = 16


def coord_pairs(target):
    place = lambda x, z, c: (x * NZ + z) * NC + c
    return [
        (place(x, z, c), place(*target(x, z, c)))
        for x in range(NX)
        for z in range(NZ)
        for c in range(NC)
    ]


def to_core(a):
    return lax.ppermute(a, "coord", coord_pairs(lambda x, z, c: (x, z, 1 - c)))


def along_x(a, d):
    return lax.ppermute(a, "coord", coord_pairs(lambda x, z, c: ((x + d) % NX, z, c)))


def swap_x(a, d):
    return lax.ppermute(a, "coord", coord_pairs(lambda x, z, c: (x ^ d, z, c)))


def swap_z(a, d):
    return lax.ppermute(a, "coord", coord_pairs(lambda x, z, c: (x, z ^ d, c)))


def swap_y(a, d):
    return lax.ppermute(a, "dp", [(y, y ^ d) for y in range(NY)])


def place_of_device():
    i = lax.axis_index("coord")
    return i // (NZ * NC), (i // NC) % NZ, i % NC


def feature_kernel(cfg, bins_hbm, h_t, g_t, h_v, g_v, proj, out_a, out_b, h_buf, g_buf, hv_buf, gv_buf, p_buf, grads, bins, sem_t, sem_v, sem_p, sem_b):
    layers, n_t, n_v, cols, blk, slots, unroll = cfg
    n = n_t + n_v
    n_a = out_a.shape[1]
    nblk = n_t // blk
    share = cols // nblk

    def train_copies(t):
        l, s = t // nblk, pl.ds((t % nblk) * blk, blk)
        at = t % slots
        return (
            pltpu.make_async_copy(h_t.at[l, s], h_buf.at[at], sem_t.at[0, at]),
            pltpu.make_async_copy(g_t.at[l, s], g_buf.at[at], sem_t.at[1, at]),
        )

    def val_copies(l):
        return (
            pltpu.make_async_copy(h_v.at[l], hv_buf.at[l], sem_v.at[0, l]),
            pltpu.make_async_copy(g_v.at[l], gv_buf.at[l], sem_v.at[1, l]),
        )

    def proj_copy(l):
        return pltpu.make_async_copy(proj.at[l], p_buf.at[l], sem_p.at[l])

    def start(copies):
        for copy in copies:
            copy.start()

    def wait(copies):
        for copy in copies:
            copy.wait()

    bins_copy = pltpu.make_async_copy(bins_hbm, bins, sem_b)
    bins_copy.start()
    for t in range(slots):
        start(train_copies(t))
        if t == 1:
            start(val_copies(0))
    proj_copy(0).start()

    @pl.loop(0, NBIN)
    def _(b):
        out_a[b] = jnp.zeros(out_a.shape[1:], jnp.float32)
        out_b[b] = jnp.zeros(out_b.shape[1:], jnp.float32)

    bins_copy.wait()
    my_x, my_z, my_c = place_of_device()

    def example(l, g, h, e):
        grads[l, pl.ds(e, cols, stride=n), :] = jnp.dot(g, h, preferred_element_type=jnp.float32)

    def project(l, j):
        a = grads[l, pl.ds(j * n, n), :].astype(jnp.bfloat16)
        p = jnp.dot(a, p_buf[l, j], preferred_element_type=jnp.float32)
        b = bins[l, j]
        far_c = (b // HALF) ^ my_c
        far_z = (b ^ my_z) & (NZ - 1)
        far_z = ((far_z ^ ((far_z >> 2) & ~(far_z >> 1))) & 1) * (NZ // 2) + far_z // 2
        b_x = b // NZ
        slot_a = ((b_x - my_x + 2) & (NX - 1)) * NZ + far_z
        slot_b = far_z * NX + ((b_x ^ my_x) & (NX - 1))
        out_a[far_c * HALF + slot_a] += p[:n_a]
        out_b[far_c * HALF + slot_b] += p[n_a:]

    for l in range(layers):

        @pl.loop(0, nblk)
        def _(b):
            t = l * nblk + b
            wait(train_copies(t))
            at = t % slots
            for i in range(blk):
                example(l, g_buf[at, i], h_buf[at, i], b * blk + i)
            if l > 0:
                for i in range(share):
                    project(l - 1, b * share + i)

            @pl.when(t + slots < layers * nblk)
            def _():
                start(train_copies(t + slots))

            if l + 1 < layers:

                @pl.when(b == nblk // 2)
                def _():
                    start(val_copies(l + 1))
                    proj_copy(l + 1).start()

        wait(val_copies(l))
        for i in range(n_v):
            example(l, gv_buf[l, i], hv_buf[l, i], n_t + i)
        proj_copy(l).wait()

    @pl.loop(0, cols, unroll=unroll)
    def _(j):
        project(layers - 1, j)


def local_features(bins, h_t, g_t, h_v, g_v, proj, n_a):
    layers, n_t, tok, r = h_t.shape
    n_v, cols = h_v.shape[1], g_t.shape[2]
    n = n_t + n_v
    blk, slots, unroll = 16, 6, 40
    in_hbm = pl.BlockSpec(memory_space=pltpu.HBM)
    return pl.pallas_call(
        functools.partial(feature_kernel, (layers, n_t, n_v, cols, blk, slots, unroll)),
        out_shape=(
            pltpu.VMEM((NBIN, n_a, BW), jnp.float32),
            pltpu.VMEM((NBIN, n - n_a, BW), jnp.float32),
        ),
        in_specs=[in_hbm] * 6,
        out_specs=[pl.BlockSpec(memory_space=pltpu.VMEM)] * 2,
        scratch_shapes=[
            pltpu.VMEM((slots, blk, tok, r), jnp.bfloat16),
            pltpu.VMEM((slots, blk, cols, tok), jnp.bfloat16),
            pltpu.VMEM((layers, n_v, tok, r), jnp.bfloat16),
            pltpu.VMEM((layers, n_v, cols, tok), jnp.bfloat16),
            pltpu.VMEM((layers, cols, r, BW), jnp.bfloat16),
            pltpu.VMEM((layers, cols * n, r), jnp.float32),
            pltpu.SMEM((layers, cols), jnp.int32),
            pltpu.SemaphoreType.DMA((2, slots)),
            pltpu.SemaphoreType.DMA((2, layers)),
            pltpu.SemaphoreType.DMA((layers,)),
            pltpu.SemaphoreType.DMA,
        ],
        compiler_params=pltpu.CompilerParams(vmem_limit_bytes=42 * 1024 * 1024),
        name="features",
    )(*[pltpu.with_memory_space_constraint(a, pltpu.HBM) for a in (bins, h_t, g_t, h_v, g_v, proj)])


def in_vmem(a):
    return pltpu.with_memory_space_constraint(a, pltpu.VMEM)


def add(parts):
    total = parts[0]
    for part in parts[1:]:
        total = total + part
    return total


def sum_quad(a):
    return add([a[0]] + [swap_z(a[i], d) for i, d in ((2, 5), (1, 2), (3, 6))])


def reduce_to_owner(f_a, f_b):
    mid = NZ // 2
    first = to_core(f_a[HALF : HALF + NZ])
    first, rest, far_b = lax.optimization_barrier((first, f_a[HALF + NZ :], f_b[HALF:]))
    far_b, rest = to_core(far_b), to_core(rest)
    half = f_a[:NZ] + first
    right, left = along_x(half[:mid], 1), along_x(half[mid:], -1)
    b = f_b[:HALF] + far_b
    far_b = swap_z(b[HALF // 2 :], 1)
    right, rest = lax.optimization_barrier((right, rest))
    half = f_a[NZ:HALF] + rest
    right = along_x(jnp.concatenate([half[2 * NZ : 2 * NZ + mid] + right, half[2 * NZ + mid :]]), 1)
    left = along_x(jnp.concatenate([half[:mid], half[mid:NZ] + left]), -1)
    b = (b[: HALF // 2] + far_b).reshape(mid, NX, *b.shape[1:])
    b = sum_quad(b)
    a = half[NZ : 2 * NZ] + right + left
    a = a[:mid] + swap_z(a[mid:], 1)
    b = add([b[0]] + [swap_x(b[d], d) for d in (2, 1, 3)])
    return sum_quad(a), b


def dots_kernel(n_v, rows_a, rows_b, v1, v2, v3, out, val):
    y = lax.axis_index("dp")
    n_b = rows_b.shape[0]
    all_v = NY * n_v
    train = rows_a[...]
    if n_b > n_v:
        train = jnp.concatenate([train, rows_b[0 : n_b - n_v, :]])
    val[pl.ds(pl.multiple_of(y * n_v, n_v), n_v), :] = rows_b[n_b - n_v : n_b, :]
    for d, part in ((1, v1), (2, v2), (3, v3)):
        val[pl.ds(pl.multiple_of((y ^ d) * n_v, n_v), n_v), :] = part[...]
    v = val[...]
    contract = lambda a, b: lax.dot_general(
        a, b, (((1,), (1,)), ((), ())), precision=lax.Precision.HIGHEST, preferred_element_type=jnp.float32
    )
    out[0:all_v, :] = contract(v, train)
    ones = jnp.ones((8, BW), jnp.float32)
    out[all_v : all_v + 8, :] = contract(ones, train * train)
    out[all_v + 8 : all_v + 16, :] = jnp.zeros((8, out.shape[1]), jnp.float32)
    out[all_v + 8 : all_v + 16, 0:all_v] = contract(ones, v * v)


def scores_kernel(*refs):
    *parts, tasks, cos_out, score_out = refs
    n_v = tasks.shape[1]
    total = add([part[...] for part in parts])
    on_diagonal = lax.broadcasted_iota(jnp.int32, (n_v, n_v), 0) == lax.broadcasted_iota(jnp.int32, (n_v, n_v), 1)
    train_norm = jnp.sqrt(total[n_v : n_v + 1, :] + 1e-06)
    val_norm_row = jnp.sqrt(total[n_v + 8 : n_v + 9, 0:n_v] + 1e-06)
    val_norm = jnp.sum(jnp.where(on_diagonal, val_norm_row, 0.0), axis=1, keepdims=True)
    cos = total[0:n_v, :] / (train_norm * val_norm)
    cos_out[...] = cos
    task_row = tasks[...].astype(jnp.float32)
    task = jnp.sum(jnp.where(on_diagonal, task_row, 0.0), axis=1, keepdims=True)
    for s in range(NTASK):
        member = (task == float(s)).astype(jnp.float32)
        count = jnp.sum(member, axis=0, keepdims=True)
        score_out[s : s + 1, :] = jnp.sum(cos * member, axis=0, keepdims=True) / count


def per_device(h_train, gout_train, h_val, gout_val, proj, bins, tasks):
    n_t, n_v = h_train.shape[1], h_val.shape[1]
    all_v = n_v * NY
    n_a = n_t - ROWS_B
    f_a, f_b = local_features(
        bins, h_train, jnp.swapaxes(gout_train, 2, 3), h_val, jnp.swapaxes(gout_val, 2, 3), proj, n_a
    )
    rows_a, rows_b = reduce_to_owner(f_a, f_b)
    v = rows_b[ROWS_B:]
    others = [swap_y(v, d) for d in (1, 2, 3)]
    a = pl.pallas_call(
        functools.partial(dots_kernel, n_v),
        out_shape=pltpu.VMEM((all_v + 16, n_t), jnp.float32),
        scratch_shapes=[pltpu.VMEM((all_v, BW), jnp.float32)],
        name="dots",
    )(*map(in_vmem, (rows_a, rows_b, *others)))
    a = add([a] + [swap_x(a, d) for d in (2, 1, 3)])
    a = add([a] + [swap_z(a, d) for d in (3, 2, 1)])
    a = a + swap_z(a, 6)
    parts = (a, to_core(a))
    cos_t, scores_t = pl.pallas_call(
        scores_kernel,
        out_shape=(
            jax.ShapeDtypeStruct((all_v, n_t), jnp.float32),
            jax.ShapeDtypeStruct((NTASK, n_t), jnp.float32),
        ),
        name="scores",
    )(*map(in_vmem, (*parts, tasks.reshape(1, all_v))))
    return cos_t.T, scores_t.T


def solution(mesh):
    in_specs = (
        P(None, "dp", None, None),
        P(None, "dp", None, "coord"),
        P(None, "dp", None, None),
        P(None, "dp", None, "coord"),
        P(None, "coord", None, None),
        P(None, "coord"),
        P(),
    )
    out_specs = (P("dp", None), P("dp", None))
    return jax.shard_map(
        per_device, mesh=mesh, in_specs=in_specs, out_specs=out_specs, check_vma=False
    )
```
